32 devices in a mesh: dp: 2 (over x), segment: 4 (over y, core), seq: 4 (over z).
Axes of the slice: x: 2, y: 2, z: 4, core: 2. Of those that a mesh axis runs over, the one named last changes fastest.
Arguments:
- layer_inputs: bfloat16 [4, 2, 512, 1024], P('segment', 'dp', 'seq'), may hold values from -24 to 24
- ln_gain: float32 [4, 1024], P('segment'), may hold values from 1 to 4
- ln_bias: float32 [4, 1024], P('segment'), may hold values from -3 to 3
- qkv_weight: bfloat16 [4, 1024, 3072], P('segment', 'dp'), may hold values from -0.1875 to 0.1875
- out_weight: bfloat16 [4, 1024, 1024], P('segment', 'dp'), may hold values from -0.1875 to 0.1875
- dec_embed: bfloat16 [1024, 512], replicated, may hold values from -0.1875 to 0.1875
- decoder_grad: bfloat16 [2, 2048, 512], P('dp', 'seq'), may hold values from -6 to 6
- previous: bfloat16 [4, 2, 512, 1024], P('segment', 'dp', 'seq'), may hold values from -6 to 6
- visible: int32 [2, 512], P('dp'), may hold values from 0 to 2047, as said below
Outputs:
- layer_grads: bfloat16 [4, 2, 512, 1024], P('segment', 'dp', 'seq')
The draws below stay inside these ranges and needn't reach their ends.
Inputs may be any that keep to these rules, and one draw needn't show every extreme that they name: `visible`: each row lists 512 distinct patch ids of one crop in ascending order. Of one crop's ids, at most 240 and at least 16 lie in any block of 512 consecutive patches (one device's block of decoder_grad), and in every crop some block holds exactly 240 and some exactly 16.
All inputs are finite; a program needn't handle non-finite values.
Results may differ from the reference program's by a relative error of at most 0.0055.
The reference program's roundings to bfloat16 on the way count: a program that leaves them out, or rounds other values in their place, can miss the bound.
Values may be sent and summed in bfloat16 or wider, within the bound.
A program may use at most 64 MiB of HBM per device.

```python
import math
import jax
import jax.numpy as jnp
from jax import lax

D = 1024
HEADS = 16
HD = 64
DEC = 512
TOK = 128
CAP = 240
VIS = 512
PATCH_DEV = 512
PATCHES = 2048
CROPS = 2
SEGMENTS = 4


def draw_layer_inputs(key, part):
    key = jax.random.fold_in(key, 11)
    first_key, second_key, third_key = jax.random.split(key, 3)
    full_shape = (SEGMENTS, CROPS, VIS, D)
    feature = jnp.exp(jax.random.uniform(second_key, (SEGMENTS, 1, 1, D), jnp.float32, math.log(0.3), math.log(3.0)))
    row_scale = jnp.exp(jax.random.uniform(third_key, (SEGMENTS, CROPS, VIS, 1), jnp.float32, math.log(0.5), math.log(2.0)))
    value = jax.random.normal(first_key, full_shape, jnp.float32) * feature * row_scale
    return jnp.clip(value, -24.0, 24.0).astype(jnp.bfloat16)


def draw_ln_gain(key, part):
    key = jax.random.fold_in(key, 7)
    low_end = 1.0
    high_end = 3.0
    value = jnp.exp(jax.random.uniform(key, (SEGMENTS, D), jnp.float32, math.log(low_end), math.log(high_end)))
    return value


def draw_visible(key, part):
    key = jax.random.fold_in(key, 5)
    regions = VIS // TOK
    half_count = regions // 2

    def region_order(region_key):
        return jax.random.permutation(region_key, PATCH_DEV)

    def one_crop(crop_key):
        first_key, second_key, third_key = jax.random.split(crop_key, 3)
        rotation = jax.random.randint(first_key, (), 0, regions)
        surplus = jax.random.randint(second_key, (half_count,), 0, TOK // 4 + 1)
        surplus = surplus.at[0].set(0)
        region_ids = jnp.arange(regions, dtype=jnp.int32)
        placed = (region_ids - rotation) % regions
        partner = placed % half_count
        crowded = placed < half_count
        counts = jnp.where(crowded, CAP - surplus[partner], 2 * TOK - CAP + surplus[partner])
        orders = jax.vmap(region_order)(jax.random.split(third_key, regions))
        positions = jnp.argsort(orders, axis=1)
        kept_flag = positions < counts[:, None]
        kept_flat = kept_flag.reshape(-1)
        sort_score = jnp.where(kept_flat, 0, PATCHES) + jnp.arange(PATCHES, dtype=jnp.int32)
        return jnp.argsort(sort_score)[:VIS].astype(jnp.int32)
    return jax.vmap(one_crop)(jax.random.split(key, CROPS))


def steps_of(rng, extent, cuts, low, top_value):
    gain, own = 1.0, jax.random.fold_in(rng, 6)
    for axis_at, blocks in cuts:
        heights = jnp.exp(jax.random.uniform(jax.random.fold_in(own, axis_at), (blocks,), jnp.float32, low / len(cuts), top_value / len(cuts)))
        gain = gain * jnp.repeat(heights, extent[axis_at] // blocks).reshape([-1 if axis == axis_at else 1 for axis in range(len(extent))])
    return gain


def normal_values(stream_key, shape, scale, most, cuts=(), kind=jnp.bfloat16):
    drawn = scale * jax.random.normal(stream_key, shape, jnp.float32)
    if cuts:
        drawn = drawn * steps_of(stream_key, shape, cuts, -0.22, 0.18)
    return jnp.clip(drawn, -most, most).astype(kind)


def setup_inputs(seed: int = 0) -> dict:
    splits = jax.random.split(jax.random.key(seed), 10)
    layer_inputs = draw_layer_inputs(jax.random.fold_in(splits[9], 71), 0)
    ln_gain = draw_ln_gain(jax.random.fold_in(splits[9], 71), 0)
    ln_bias = normal_values(splits[2], (SEGMENTS, D), 0.5, 3.0, ((0, 4),), jnp.float32)
    qkv_weight = normal_values(splits[3], (SEGMENTS, D, 3 * D), D ** -0.5, 0.1875, ((0, 4), (1, 2)))
    out_weight = normal_values(splits[4], (SEGMENTS, D, D), D ** -0.5, 0.1875, ((0, 4), (1, 2)))
    dec_embed = normal_values(splits[5], (D, DEC), D ** -0.5, 0.1875)
    decoder_grad = normal_values(splits[6], (CROPS, PATCHES, DEC), 1.0, 6.0, ((0, 2), (1, 4)))
    previous = normal_values(splits[7], (SEGMENTS, CROPS, VIS, D), 1.0, 6.0, ((0, 4), (1, 2), (2, 4)))
    visible = draw_visible(jax.random.fold_in(splits[9], 71), 0)
    return {"layer_inputs": layer_inputs, "ln_gain": ln_gain, "ln_bias": ln_bias, "qkv_weight": qkv_weight, "out_weight": out_weight, "dec_embed": dec_embed, "decoder_grad": decoder_grad, "previous": previous, "visible": visible}


eps_norm = 1e-06

def contract_last(left_side, right_side):
    return lax.dot_general(left_side, right_side, (((1,), (1,)), ((), ())), preferred_element_type=jnp.float32)

def contract_first(left_side, right_side):
    return lax.dot_general(left_side, right_side, (((0,), (0,)), ((), ())), preferred_element_type=jnp.float32)

def head_backward(sections):
    query_rows, key_rows, value_rows, grad_out = sections
    scaling = HD ** (-0.5)
    scores = contract_last(query_rows, key_rows) * scaling
    row_top = lax.optimization_barrier(jnp.max(scores, axis=1, keepdims=True))
    weights = jnp.exp(scores - row_top)
    probability = weights / lax.optimization_barrier(jnp.sum(weights, axis=1, keepdims=True))
    prob_low = probability.astype(jnp.bfloat16)
    output = jnp.dot(prob_low, value_rows, preferred_element_type=jnp.float32)
    row_delta = lax.optimization_barrier(jnp.sum(grad_out.astype(jnp.float32) * output, axis=1, keepdims=True))
    grad_probs = contract_last(grad_out, value_rows)
    grad_scores = (probability * (grad_probs - row_delta)).astype(jnp.bfloat16)
    query_grad = (jnp.dot(grad_scores, key_rows, preferred_element_type=jnp.float32) * scaling).astype(jnp.bfloat16)
    key_grad = (contract_first(grad_scores, query_rows) * scaling).astype(jnp.bfloat16)
    value_grad = contract_first(prob_low, grad_out).astype(jnp.bfloat16)
    return (query_grad, key_grad, value_grad)

def layer_backward(tokens, norm_gain, norm_bias, qkv_full, out_full, cotangent):
    values = tokens.astype(jnp.float32)
    center = values - lax.optimization_barrier(jnp.mean(values, axis=1, keepdims=True))
    spread = jnp.sqrt(lax.optimization_barrier(jnp.mean(center * center, axis=1, keepdims=True)) + eps_norm)
    normed = center / spread
    lowered = (normed * norm_gain + norm_bias).astype(jnp.bfloat16)
    projected = jnp.dot(lowered, qkv_full, preferred_element_type=jnp.float32).astype(jnp.bfloat16)
    grad_attn = contract_last(cotangent, out_full).astype(jnp.bfloat16)
    sections = projected.reshape(VIS, 3, HEADS, HD).transpose(1, 2, 0, 3)
    head_grads = grad_attn.reshape(VIS, HEADS, HD).transpose(1, 0, 2)
    query_grad, key_grad, value_grad = lax.map(head_backward, (sections[0], sections[1], sections[2], head_grads))
    grad_proj = jnp.stack([query_grad, key_grad, value_grad], axis=0).transpose(2, 0, 1, 3).reshape(VIS, 3 * D)
    grad_norm = contract_last(grad_proj, qkv_full)
    scaled = grad_norm * norm_gain
    grad_in = (scaled - lax.optimization_barrier(jnp.mean(scaled, axis=1, keepdims=True)) - normed * lax.optimization_barrier(jnp.mean(scaled * normed, axis=1, keepdims=True))) / spread
    return (cotangent.astype(jnp.float32) + grad_in).astype(jnp.bfloat16)

def pick_rows(patch_grid, patch_ids):
    return jnp.take(patch_grid, patch_ids, axis=0)

def reference(layer_inputs, ln_gain, ln_bias, qkv_weight, out_weight, dec_embed, decoder_grad, previous, visible):
    picked_rows = jax.vmap(pick_rows)(decoder_grad, visible)
    returned = contract_last(picked_rows.reshape(CROPS * VIS, DEC), dec_embed).astype(jnp.bfloat16).reshape(CROPS, VIS, D)
    cotangents = jnp.concatenate([previous[1:], returned[None]], axis=0)

    def one_segment(segment_items):
        tokens, norm_gain, norm_bias, qkv_full, out_full, segment_cots = segment_items

        def one_crop(couple):
            return layer_backward(couple[0], norm_gain, norm_bias, qkv_full, out_full, couple[1])
        return lax.map(one_crop, (tokens, segment_cots))
    return lax.map(one_segment, (layer_inputs, ln_gain, ln_bias, qkv_weight, out_weight, cotangents))
```

```python
import functools

import jax
import jax.numpy as jnp
from jax import lax
from jax.experimental import pallas as pl
from jax.experimental.pallas import tpu as pltpu
from jax.sharding import PartitionSpec as P

HEADS = 16
EPS = 1e-06
MESH = pl.DeviceIdType.MESH
F32 = jnp.float32
BF16 = jnp.bfloat16


def contract_last(left_side, right_side):
    return lax.dot_general(
        left_side, right_side, (((1,), (1,)), ((), ())), preferred_element_type=F32
    )


def contract_first(left_side, right_side):
    return lax.dot_general(
        left_side, right_side, (((0,), (0,)), ((), ())), preferred_element_type=F32
    )


def head_backward(query_rows, key_rows, value_rows, grad_out, scaling):
    rows = query_rows.shape[0]
    step = min(512, rows)
    query_grads = []
    key_grad = value_grad = None
    for at in range(0, rows, step):
        query = query_rows[at : at + step]
        grad = grad_out[at : at + step]
        scores = contract_last(query, key_rows) * scaling
        weights = jnp.exp(scores - jnp.max(scores, axis=1, keepdims=True))
        probs = weights * (1.0 / jnp.sum(weights, axis=1, keepdims=True))
        probs_low = probs.astype(BF16)
        output = jnp.dot(probs_low, value_rows, preferred_element_type=F32)
        row_delta = jnp.sum(grad.astype(F32) * output, axis=1, keepdims=True)
        grad_probs = contract_last(grad, value_rows)
        grad_scores = (probs * (grad_probs - row_delta)).astype(BF16)
        query_grads.append(
            (jnp.dot(grad_scores, key_rows, preferred_element_type=F32) * scaling).astype(BF16)
        )
        key_part = contract_first(grad_scores, query) * scaling
        value_part = contract_first(probs_low, grad)
        key_grad = key_part if key_grad is None else key_grad + key_part
        value_grad = value_part if value_grad is None else value_grad + value_part
    query_grad = query_grads[0] if len(query_grads) == 1 else jnp.concatenate(query_grads, axis=0)
    return query_grad, key_grad.astype(BF16), value_grad.astype(BF16)


def kernel(
    dims,
    x_ref, gain_ref, bias_ref, prev_ref, ids_ref, w_ref, ow_ref, de_ref, dg_ref,
    out_ref,
    wg, wc, ow, de, dg, low, normed_ref, spread_ref, cot, go, ga, pk, pr,
    pj, gp, rb, gns, gnr,
    lw_sem, lo_sem, prev_s, prev_r, w_s, w_r, pk_s, pk_r, l_s, l_r, ct_s, ct_r,
    g_s, g_r, b_s, b_r, f_s, f_r, n_s, n_r,
):
    dp, segs, groups, tok, width, chunks, pair, head_size, sliced = dims
    cw = pair * head_size
    hw = chunks * cw
    depth = width // dp
    per_dp = groups // dp
    d = lax.axis_index("dp")
    s = lax.axis_index("segment")
    z = lax.axis_index("seq")
    last = s == segs - 1
    owner = z // per_dp

    def z_at(o):
        return lax.rem(z + o, groups)

    def d_at(o):
        return lax.rem(d + o, dp)

    def remote(src, dst, send, recv, dd, ss, zz):
        return pltpu.make_async_remote_copy(
            src_ref=src, dst_ref=dst, send_sem=send, recv_sem=recv,
            device_id=(dd, ss, zz), device_id_type=MESH,
        )

    def w_copies(o):
        g = z_at(o)
        if not sliced:
            return [pltpu.make_async_copy(w_ref.at[g], wg.at[g], lw_sem.at[o, 0, 0])]
        found = []
        for ch in range(chunks):
            for part in range(3):
                at = pl.multiple_of(part * width + g * hw + ch * cw, 128)
                found.append(
                    pltpu.make_async_copy(
                        w_ref.at[:, pl.ds(at, cw)],
                        wg.at[g, ch, :, pl.ds(part * cw, cw)],
                        lw_sem.at[o, ch, part],
                    )
                )
        return found

    local_w = [w_copies(o) for o in range(groups)]
    ow_copy = pltpu.make_async_copy(ow_ref, ow, lo_sem.at[0])
    de_copy = pltpu.make_async_copy(de_ref, de, lo_sem.at[1])
    dg_copy = pltpu.make_async_copy(dg_ref, dg, lo_sem.at[2])
    for copy in local_w[0]:
        copy.start()

    @pl.when(last)
    def _():
        dg_copy.start()
        de_copy.start()

    ow_copy.start()
    for o in range(1, groups):
        for copy in local_w[o]:
            copy.start()

    barrier = pltpu.get_barrier_semaphore()
    for od in range(dp):
        for oz in range(groups):
            if od or oz:
                pl.semaphore_signal(
                    barrier, inc=1, device_id=(d_at(od), s, z_at(oz)), device_id_type=MESH
                )

    pl.semaphore_signal(
        barrier, inc=1, device_id=(d, lax.rem(s + 1, segs), z), device_id_type=MESH
    )
    pl.semaphore_wait(barrier, dp * groups)

    down = jnp.maximum(s - 1, 0)
    prev_copy = remote(prev_ref, cot.at[d], prev_s.at[0], prev_r.at[0], d, down, z)

    @pl.when(s > 0)
    def _():
        prev_copy.start()

    def pick_copy(o):
        g = z_at(o)
        return remote(pk.at[g], pr.at[z], pk_s.at[g], pk_r.at[z], d, s, g)

    def arrive(dst, recv, dd, zz):
        remote(dst, dst, recv, recv, dd, s, zz).wait_recv()

    @pl.when(last)
    def _():
        dg_copy.wait()
        patches = dg.shape[0]
        patch_ids = lax.broadcasted_iota(jnp.int32, (patches, tok), 0) + z * patches
        for o in list(range(1, groups)) + [0]:
            g = z_at(o)
            hit = jnp.where(patch_ids == ids_ref[g], 1.0, 0.0).astype(BF16)
            rows = contract_first(hit, dg[...]).astype(BF16)
            if o:
                pk[g] = rows
                pick_copy(o).start()
            else:
                pr[z] = rows

    values = x_ref[...].astype(F32)
    center = values - jnp.mean(values, axis=1, keepdims=True)
    spread = jnp.sqrt(jnp.mean(center * center, axis=1, keepdims=True) + EPS)
    normed = center / spread
    normed_ref[...] = normed
    spread_ref[...] = jnp.broadcast_to(spread, spread_ref.shape)
    low[z] = (normed * gain_ref[...] + bias_ref[...]).astype(BF16)

    def low_copy(o):
        return remote(low.at[z], low.at[z], l_s.at[z_at(o)], l_r.at[z], d, s, z_at(o))

    for o in range(1, groups):
        low_copy(o).start()

    def w_copy(o, ch):
        dd = d_at(o)
        return remote(wg.at[z, ch], wc.at[d, ch], w_s.at[dd, ch], w_r.at[d, ch], dd, s, z)

    for copy in local_w[0]:
        copy.wait()
    for ch in range(chunks):
        for o in range(1, dp):
            w_copy(o, ch).start()

    @pl.when(s < segs - 1)
    def _():
        prev_copy.wait_recv()

    @pl.when(last)
    def _():
        for o in range(1, groups):
            arrive(pr.at[z_at(o)], pk_r.at[z_at(o)], d, z_at(o))
        picked = pr[0].astype(F32)
        for g in range(1, groups):
            picked = picked + pr[g].astype(F32)
        de_copy.wait()
        cot[d] = contract_last(picked.astype(BF16), de[...]).astype(BF16)

    def cot_copy(o):
        return remote(cot.at[d], cot.at[d], ct_s.at[d_at(o)], ct_r.at[d], d_at(o), s, z)

    for o in range(1, dp):
        cot_copy(o).start()

    def g_copy(c, j):
        g = d * per_dp + j
        return remote(go.at[c, j], ga.at[z], g_s.at[c, j], g_r.at[z], c, s, g)

    ow_copy.wait()
    for o in range(dp):
        c = d_at(o)
        if o:
            arrive(cot.at[c], ct_r.at[c], c, z)
        grads = contract_last(cot[c], ow[...]).astype(BF16)
        for j in range(per_dp):
            for ch in range(chunks):
                at = (j * chunks + ch) * cw
                go[c, j, ch] = grads[:, at : at + cw]
            if o:
                g_copy(c, j).start()
            else:
                mine = d * per_dp + j == z

                @pl.when(jnp.logical_not(mine))
                def _():
                    g_copy(c, j).start()

                @pl.when(mine)
                def _():
                    ga[z] = go[c, j]

    def back_copy(o, ch):
        g = z_at(o)
        return remote(gp.at[ch, g], rb.at[ch, d, z], b_s.at[ch, g], b_r.at[ch, z], d, s, g)

    def forward_copy(o, ch, g):
        dd = d_at(o)
        return remote(
            rb.at[ch, d, g], rb.at[ch, d, g], f_s.at[ch, dd, g], f_r.at[ch, d, g], dd, s, z
        )

    def forward(ch):
        for o in range(1, groups):
            g = z_at(o)
            arrive(rb.at[ch, d, g], b_r.at[ch, g], d, g)
            for od in range(1, dp):
                forward_copy(od, ch, g).start()

    scaling = head_size ** (-0.5)
    for ch in range(chunks):
        if ch == 0:
            for o in range(1, groups):
                arrive(low.at[z_at(o)], l_r.at[z_at(o)], d, z_at(o))
        total = None
        for o in range(dp):
            dd = d_at(o)
            if o:
                arrive(wc.at[dd, ch], w_r.at[dd, ch], dd, z)
            weights = wc[dd, ch] if o else wg[z, ch]
            columns = low[:, :, pl.ds(pl.multiple_of(dd * depth, depth), depth)]
            term = jnp.dot(
                columns.reshape(groups * tok, depth), weights, preferred_element_type=F32
            )
            total = term if total is None else total + term
        pj[...] = total.astype(BF16)
        if ch == 0:
            for src in range(groups):
                @pl.when(jnp.logical_not(jnp.logical_and(owner == d, src == z)))
                def _():
                    arrive(ga.at[src], g_r.at[src], owner, src)
        grad_rows = ga[:, ch].reshape(groups * tok, cw)
        found = ([], [], [])
        for h in range(pair):
            parts = [
                pj[:, part * cw + h * head_size : part * cw + (h + 1) * head_size]
                for part in range(3)
            ]
            result = head_backward(
                *parts, grad_rows[:, h * head_size : (h + 1) * head_size], scaling
            )
            for part in range(3):
                found[part].append(result[part])
        for part in range(3):
            whole = found[part][0] if pair == 1 else jnp.concatenate(found[part], axis=1)
            gp[ch, :, :, part * cw : (part + 1) * cw] = whole.reshape(groups, tok, cw)
        for o in range(1, groups):
            back_copy(o, ch).start()
        rb[ch, d, z] = gp[ch, z]
        for od in range(1, dp):
            forward_copy(od, ch, z).start()
        if ch:
            forward(ch - 1)
    forward(chunks - 1)
    for o in range(1, groups):
        for copy in local_w[o]:
            copy.wait()

    def half(c):
        def step(g, total):
            for ch in range(chunks):
                total = total + contract_last(rb[ch, c, g], wg[g, ch])
            return total

        return lax.fori_loop(0, groups, step, jnp.zeros((tok, depth), F32))

    def n_copy(o):
        c = d_at(o)
        return remote(gns.at[c], gnr.at[d], n_s.at[c], n_r.at[d], c, s, z)

    gnr[d] = half(d)
    for o in range(1, dp):
        c = d_at(o)
        for ch in range(chunks):
            for g in range(groups):
                arrive(rb.at[ch, c, g], f_r.at[ch, c, g], c, z)
        gns[c] = half(c)
        n_copy(o).start()
    for o in range(1, dp):
        arrive(gnr.at[d_at(o)], n_r.at[d_at(o)], d_at(o), z)
    grad_norm = jnp.concatenate([gnr[c] for c in range(dp)], axis=1)
    scaled = grad_norm * gain_ref[...]
    normed = normed_ref[...]
    grad_in = (
        scaled
        - jnp.mean(scaled, axis=1, keepdims=True)
        - normed * jnp.mean(scaled * normed, axis=1, keepdims=True)
    ) / spread_ref[:, :1]
    out_ref[...] = (cot[d].astype(F32) + grad_in).astype(BF16)

    @pl.when(s > 0)
    def _():
        prev_copy.wait_send()

    @pl.when(last)
    def _():
        for o in range(1, groups):
            pick_copy(o).wait_send()

    for o in range(1, groups):
        low_copy(o).wait_send()
        for ch in range(chunks):
            back_copy(o, ch).wait_send()
    for o in range(1, dp):
        cot_copy(o).wait_send()
        n_copy(o).wait_send()
        for ch in range(chunks):
            w_copy(o, ch).wait_send()
            for g in range(groups):
                forward_copy(o, ch, g).wait_send()
    for o in range(dp):
        c = d_at(o)
        for j in range(per_dp):
            if o:
                g_copy(c, j).wait_send()
            else:
                @pl.when(d * per_dp + j != z)
                def _():
                    g_copy(c, j).wait_send()


def on_device(
    layer_inputs, ln_gain, ln_bias, qkv_weight, out_weight, dec_embed, decoder_grad, previous, visible
):
    dp = lax.axis_size("dp")
    segs = lax.axis_size("segment")
    groups = lax.axis_size("seq")
    tokens = layer_inputs[0, 0]
    tok, width = tokens.shape
    head_size = width // HEADS
    head_count = HEADS // groups
    pair = 2 if head_count % 2 == 0 else 1
    chunks = head_count // pair
    cw = pair * head_size
    depth = width // dp
    per_dp = groups // dp
    patches, dec = decoder_grad.shape[1:]
    sliced = cw % 128 == 0
    weight = qkv_weight[0]
    if not sliced:
        weight = weight.reshape(depth, 3, groups, chunks, cw).transpose(2, 3, 0, 1, 4)
        weight = weight.reshape(groups, chunks, depth, 3 * cw)
    dims = (dp, segs, groups, tok, width, chunks, pair, head_size, sliced)
    vmem = pl.BlockSpec(memory_space=pltpu.VMEM)
    anywhere = pl.BlockSpec(memory_space=pl.ANY)
    dma = pltpu.SemaphoreType.DMA
    result = pl.pallas_call(
        functools.partial(kernel, dims),
        out_shape=jax.ShapeDtypeStruct((tok, width), BF16),
        in_specs=[vmem] * 5 + [anywhere] * 4,
        out_specs=vmem,
        scratch_shapes=[
            pltpu.VMEM((groups, chunks, depth, 3 * cw), BF16),
            pltpu.VMEM((dp, chunks, depth, 3 * cw), BF16),
            pltpu.VMEM((depth, width), BF16),
            pltpu.VMEM((width, dec), BF16),
            pltpu.VMEM((patches, dec), BF16),
            pltpu.VMEM((groups, tok, width), BF16),
            pltpu.VMEM((tok, width), F32),
            pltpu.VMEM((tok, 128), F32),
            pltpu.VMEM((dp, tok, width), BF16),
            pltpu.VMEM((dp, per_dp, chunks, tok, cw), BF16),
            pltpu.VMEM((groups, chunks, tok, cw), BF16),
            pltpu.VMEM((groups, tok, dec), BF16),
            pltpu.VMEM((groups, tok, dec), BF16),
            pltpu.VMEM((groups * tok, 3 * cw), BF16),
            pltpu.VMEM((chunks, groups, tok, 3 * cw), BF16),
            pltpu.VMEM((chunks, dp, groups, tok, 3 * cw), BF16),
            pltpu.VMEM((dp, tok, depth), F32),
            pltpu.VMEM((dp, tok, depth), F32),
            dma((groups, chunks, 3)),
            dma((3,)),
            dma((1,)),
            dma((1,)),
            dma((dp, chunks)),
            dma((dp, chunks)),
            dma((groups,)),
            dma((groups,)),
            dma((groups,)),
            dma((groups,)),
            dma((dp,)),
            dma((dp,)),
            dma((dp, per_dp)),
            dma((groups,)),
            dma((chunks, groups)),
            dma((chunks, groups)),
            dma((chunks, dp, groups)),
            dma((chunks, dp, groups)),
            dma((dp,)),
            dma((dp,)),
        ],
        compiler_params=pltpu.CompilerParams(
            collective_id=0, has_side_effects=True, vmem_limit_bytes=56 * 1024 * 1024
        ),
    )(
        tokens,
        ln_gain,
        ln_bias,
        previous[0, 0],
        visible[0].reshape(groups, 1, tok),
        weight,
        out_weight[0],
        dec_embed,
        decoder_grad[0],
    )
    return result[None, None]


def solution(mesh):
    placed = (
        P("segment", "dp", "seq", None),
        P("segment", None),
        P("segment", None),
        P("segment", "dp", None),
        P("segment", "dp", None),
        P(),
        P("dp", "seq", None),
        P("segment", "dp", "seq", None),
        P("dp", None),
    )
    return jax.shard_map(
        on_device,
        mesh=mesh,
        in_specs=placed,
        out_specs=P("segment", "dp", "seq", None),
        check_vma=False,
    )
```

```python
import functools

import jax
import jax.numpy as jnp
from jax import lax
from jax.experimental import pallas as pl
from jax.experimental.pallas import tpu as pltpu
from jax.sharding import PartitionSpec as P

HEADS = 16
EPS = 1e-06
MESH = pl.DeviceIdType.MESH
F32 = jnp.float32
BF16 = jnp.bfloat16


def contract_last(left_side, right_side):
    return lax.dot_general(
        left_side, right_side, (((1,), (1,)), ((), ())), preferred_element_type=F32
    )


def contract_first(left_side, right_side):
    return lax.dot_general(
        left_side, right_side, (((0,), (0,)), ((), ())), preferred_element_type=F32
    )


def head_backward(query_rows, key_rows, value_rows, grad_out, scaling):
    rows = query_rows.shape[0]
    step = min(512, rows)
    query_grads = []
    key_grad = value_grad = None
    for at in range(0, rows, step):
        query = query_rows[at : at + step]
        grad = grad_out[at : at + step]
        scores = contract_last(query, key_rows) * scaling
        weights = jnp.exp(scores - jnp.max(scores, axis=1, keepdims=True))
        probs = weights * (1.0 / jnp.sum(weights, axis=1, keepdims=True))
        probs_low = probs.astype(BF16)
        output = jnp.dot(probs_low, value_rows, preferred_element_type=F32)
        row_delta = jnp.sum(grad.astype(F32) * output, axis=1, keepdims=True)
        grad_probs = contract_last(grad, value_rows)
        grad_scores = (probs * (grad_probs - row_delta)).astype(BF16)
        query_grads.append(
            (jnp.dot(grad_scores, key_rows, preferred_element_type=F32) * scaling).astype(BF16)
        )
        key_part = contract_first(grad_scores, query) * scaling
        value_part = contract_first(probs_low, grad)
        key_grad = key_part if key_grad is None else key_grad + key_part
        value_grad = value_part if value_grad is None else value_grad + value_part
    query_grad = query_grads[0] if len(query_grads) == 1 else jnp.concatenate(query_grads, axis=0)
    return query_grad, key_grad.astype(BF16), value_grad.astype(BF16)


def kernel(
    dims,
    x_ref, gain_ref, bias_ref, prev_ref, ids_ref, w_ref, ow_ref, de_ref, dg_ref,
    out_ref,
    wc, ow, de, dg, low, normed_ref, spread_ref, cot, go, ga, pk, pr, px,
    pj, gp, ps, pn,
    lw_sem, lo_sem, prev_s, prev_r, w_s, w_r, pk_s, pk_r, px_s, px_r, l_s, l_r,
    g_s, g_r, b_s, b_r,
):
    dp, segs, groups, tok, width, chunks, pair, head_size, sliced = dims
    cw = pair * head_size
    hw = chunks * cw
    depth = width // dp
    per_dp = groups // dp
    d = lax.axis_index("dp")
    s = lax.axis_index("segment")
    z = lax.axis_index("seq")
    last = s == segs - 1
    owner = z // per_dp

    def z_at(o):
        return lax.rem(z + o, groups)

    def d_at(o):
        return lax.rem(d + o, dp)

    def remote(src, dst, send, recv, dd, ss, zz):
        return pltpu.make_async_remote_copy(
            src_ref=src, dst_ref=dst, send_sem=send, recv_sem=recv,
            device_id=(dd, ss, zz), device_id_type=MESH,
        )

    local_w = []
    if sliced:
        for ch in range(chunks):
            for part in range(3):
                at = pl.multiple_of(part * width + z * hw + ch * cw, 128)
                local_w.append(
                    pltpu.make_async_copy(
                        w_ref.at[:, pl.ds(at, cw)],
                        wc.at[d, ch, :, pl.ds(part * cw, cw)],
                        lw_sem.at[ch, part],
                    )
                )
    else:
        local_w.append(pltpu.make_async_copy(w_ref.at[z], wc.at[d], lw_sem.at[0, 0]))
    ow_copy = pltpu.make_async_copy(ow_ref, ow, lo_sem.at[0])
    de_copy = pltpu.make_async_copy(de_ref, de, lo_sem.at[1])
    dg_copy = pltpu.make_async_copy(dg_ref, dg, lo_sem.at[2])
    for copy in local_w:
        copy.start()

    @pl.when(last)
    def _():
        dg_copy.start()
        de_copy.start()

    ow_copy.start()

    barrier = pltpu.get_barrier_semaphore()
    for od in range(dp):
        for oz in range(groups):
            if od or oz:
                pl.semaphore_signal(
                    barrier, inc=1, device_id=(d_at(od), s, z_at(oz)), device_id_type=MESH
                )

    for od in range(dp):
        pl.semaphore_signal(
            barrier, inc=1, device_id=(d_at(od), lax.rem(s + 1, segs), z), device_id_type=MESH
        )
    pl.semaphore_wait(barrier, dp * groups - 1 + dp)

    down = jnp.maximum(s - 1, 0)

    def prev_copy(o):
        c = d_at(o)
        return remote(prev_ref, cot.at[d], prev_s.at[c], prev_r.at[d], c, down, z)

    @pl.when(s > 0)
    def _():
        for o in range(dp):
            prev_copy(o).start()

    def pick_copy(o):
        g = z_at(o)
        return remote(pk.at[g], pr.at[z], pk_s.at[g], pk_r.at[z], d, s, g)

    def arrive(dst, recv, dd, zz):
        remote(dst, dst, recv, recv, dd, s, zz).wait_recv()

    @pl.when(last)
    def _():
        dg_copy.wait()
        patches = dg.shape[0]
        patch_ids = lax.broadcasted_iota(jnp.int32, (patches, tok), 0) + z * patches
        for o in list(range(1, groups)) + [0]:
            g = z_at(o)
            hit = jnp.where(patch_ids == ids_ref[g], 1.0, 0.0).astype(BF16)
            rows = contract_first(hit, dg[...]).astype(BF16)
            if o:
                pk[g] = rows
                pick_copy(o).start()
            else:
                pr[z] = rows

    values = x_ref[...].astype(F32)
    center = values - jnp.mean(values, axis=1, keepdims=True)
    spread = jnp.sqrt(jnp.mean(center * center, axis=1, keepdims=True) + EPS)
    normed = center / spread
    normed_ref[...] = normed
    spread_ref[...] = jnp.broadcast_to(spread, spread_ref.shape)
    low[z] = (normed * gain_ref[...] + bias_ref[...]).astype(BF16)

    def low_copy(o):
        return remote(low.at[z], low.at[z], l_s.at[z_at(o)], l_r.at[z], d, s, z_at(o))

    for o in range(1, groups):
        low_copy(o).start()

    def w_copy(o, ch):
        dd = d_at(o)
        return remote(wc.at[d, ch], wc.at[d, ch], w_s.at[dd, ch], w_r.at[d, ch], dd, s, z)

    for copy in local_w:
        copy.wait()
    for ch in range(chunks):
        for o in range(1, dp):
            w_copy(o, ch).start()

    def px_copy(o):
        return remote(px.at[d], px.at[d], px_s.at[d_at(o)], px_r.at[d], d_at(o), s, z)

    @pl.when(last)
    def _():
        for o in range(1, groups):
            arrive(pr.at[z_at(o)], pk_r.at[z_at(o)], d, z_at(o))
        picked = pr[0].astype(F32)
        for g in range(1, groups):
            picked = picked + pr[g].astype(F32)
        px[d] = picked.astype(BF16)
        for o in range(1, dp):
            px_copy(o).start()
        de_copy.wait()

    def g_copy(c, j):
        g = d * per_dp + j
        return remote(go.at[c, j], ga.at[z], g_s.at[c, j], g_r.at[z], c, s, g)

    ow_copy.wait()
    for o in range(dp):
        c = d_at(o)

        @pl.when(s < segs - 1)
        def _():
            remote(
                prev_ref, cot.at[c], prev_s.at[c], prev_r.at[c], c, lax.rem(s + 1, segs), z
            ).wait_recv()

        @pl.when(last)
        def _():
            if o:
                arrive(px.at[c], px_r.at[c], c, z)
            cot[c] = contract_last(px[c], de[...]).astype(BF16)

        grads = contract_last(cot[c], ow[...]).astype(BF16)
        for j in range(per_dp):
            for ch in range(chunks):
                at = (j * chunks + ch) * cw
                go[c, j, ch] = grads[:, at : at + cw]
            if o:
                g_copy(c, j).start()
            else:
                mine = d * per_dp + j == z

                @pl.when(jnp.logical_not(mine))
                def _():
                    g_copy(c, j).start()

                @pl.when(mine)
                def _():
                    ga[z] = go[c, j]

    def back_copy(o):
        g = z_at(o)
        return remote(ps.at[g], pn.at[z], b_s.at[g], b_r.at[z], d, s, g)

    scaling = head_size ** (-0.5)
    for ch in range(chunks):
        if ch == 0:
            for o in range(1, groups):
                arrive(low.at[z_at(o)], l_r.at[z_at(o)], d, z_at(o))
        total = None
        for o in range(dp):
            dd = d_at(o)
            if o:
                arrive(wc.at[dd, ch], w_r.at[dd, ch], dd, z)
            weights = wc[dd, ch]
            columns = low[:, :, pl.ds(pl.multiple_of(dd * depth, depth), depth)]
            term = jnp.dot(
                columns.reshape(groups * tok, depth), weights, preferred_element_type=F32
            )
            total = term if total is None else total + term
        pj[...] = total.astype(BF16)
        if ch == 0:
            for src in range(groups):
                @pl.when(jnp.logical_not(jnp.logical_and(owner == d, src == z)))
                def _():
                    arrive(ga.at[src], g_r.at[src], owner, src)
        grad_rows = ga[:, ch].reshape(groups * tok, cw)
        found = ([], [], [])
        for h in range(pair):
            parts = [
                pj[:, part * cw + h * head_size : part * cw + (h + 1) * head_size]
                for part in range(3)
            ]
            result = head_backward(
                *parts, grad_rows[:, h * head_size : (h + 1) * head_size], scaling
            )
            for part in range(3):
                found[part].append(result[part])
        for part in range(3):
            whole = found[part][0] if pair == 1 else jnp.concatenate(found[part], axis=1)
            gp[ch, :, :, part * cw : (part + 1) * cw] = whole.reshape(groups, tok, cw)

    def term(g, c):
        total = None
        for ch in range(chunks):
            part = contract_last(gp[ch, g], wc[c, ch])
            total = part if total is None else total + part
        return total

    for o in range(1, groups):
        g = z_at(o)
        for c in range(dp):
            ps[g, :, c * depth : (c + 1) * depth] = term(g, c).astype(BF16)
        back_copy(o).start()
    grad_norm = jnp.concatenate([term(z, c) for c in range(dp)], axis=1)
    for o in range(1, groups):
        g = z_at(o)
        arrive(pn.at[g], b_r.at[g], d, g)
        grad_norm = grad_norm + pn[g].astype(F32)
    scaled = grad_norm * gain_ref[...]
    normed = normed_ref[...]
    grad_in = (
        scaled
        - jnp.mean(scaled, axis=1, keepdims=True)
        - normed * jnp.mean(scaled * normed, axis=1, keepdims=True)
    ) / spread_ref[:, :1]
    out_ref[...] = (cot[d].astype(F32) + grad_in).astype(BF16)

    @pl.when(s > 0)
    def _():
        for o in range(dp):
            prev_copy(o).wait_send()

    @pl.when(last)
    def _():
        for o in range(1, groups):
            pick_copy(o).wait_send()
        for o in range(1, dp):
            px_copy(o).wait_send()

    for o in range(1, groups):
        low_copy(o).wait_send()
        back_copy(o).wait_send()
    for o in range(1, dp):
        for ch in range(chunks):
            w_copy(o, ch).wait_send()
    for o in range(dp):
        c = d_at(o)
        for j in range(per_dp):
            if o:
                g_copy(c, j).wait_send()
            else:
                @pl.when(d * per_dp + j != z)
                def _():
                    g_copy(c, j).wait_send()


def on_device(
    layer_inputs, ln_gain, ln_bias, qkv_weight, out_weight, dec_embed, decoder_grad, previous, visible
):
    dp = lax.axis_size("dp")
    segs = lax.axis_size("segment")
    groups = lax.axis_size("seq")
    tokens = layer_inputs[0, 0]
    tok, width = tokens.shape
    head_size = width // HEADS
    head_count = HEADS // groups
    pair = 2 if head_count % 2 == 0 else 1
    chunks = head_count // pair
    cw = pair * head_size
    depth = width // dp
    per_dp = groups // dp
    patches, dec = decoder_grad.shape[1:]
    sliced = cw % 128 == 0
    weight = qkv_weight[0]
    if not sliced:
        weight = weight.reshape(depth, 3, groups, chunks, cw).transpose(2, 3, 0, 1, 4)
        weight = weight.reshape(groups, chunks, depth, 3 * cw)
    dims = (dp, segs, groups, tok, width, chunks, pair, head_size, sliced)
    vmem = pl.BlockSpec(memory_space=pltpu.VMEM)
    anywhere = pl.BlockSpec(memory_space=pl.ANY)
    dma = pltpu.SemaphoreType.DMA
    result = pl.pallas_call(
        functools.partial(kernel, dims),
        out_shape=jax.ShapeDtypeStruct((tok, width), BF16),
        in_specs=[vmem] * 5 + [anywhere] * 4,
        out_specs=vmem,
        scratch_shapes=[
            pltpu.VMEM((dp, chunks, depth, 3 * cw), BF16),
            pltpu.VMEM((depth, width), BF16),
            pltpu.VMEM((width, dec), BF16),
            pltpu.VMEM((patches, dec), BF16),
            pltpu.VMEM((groups, tok, width), BF16),
            pltpu.VMEM((tok, width), F32),
            pltpu.VMEM((tok, 128), F32),
            pltpu.VMEM((dp, tok, width), BF16),
            pltpu.VMEM((dp, per_dp, chunks, tok, cw), BF16),
            pltpu.VMEM((groups, chunks, tok, cw), BF16),
            pltpu.VMEM((groups, tok, dec), BF16),
            pltpu.VMEM((groups, tok, dec), BF16),
            pltpu.VMEM((dp, tok, dec), BF16),
            pltpu.VMEM((groups * tok, 3 * cw), BF16),
            pltpu.VMEM((chunks, groups, tok, 3 * cw), BF16),
            pltpu.VMEM((groups, tok, width), BF16),
            pltpu.VMEM((groups, tok, width), BF16),
            dma((chunks, 3)),
            dma((3,)),
            dma((dp,)),
            dma((dp,)),
            dma((dp, chunks)),
            dma((dp, chunks)),
            dma((groups,)),
            dma((groups,)),
            dma((dp,)),
            dma((dp,)),
            dma((groups,)),
            dma((groups,)),
            dma((dp, per_dp)),
            dma((groups,)),
            dma((groups,)),
            dma((groups,)),
        ],
        compiler_params=pltpu.CompilerParams(
            collective_id=0, has_side_effects=True, vmem_limit_bytes=56 * 1024 * 1024
        ),
    )(
        tokens,
        ln_gain,
        ln_bias,
        previous[0, 0],
        visible[0].reshape(groups, 1, tok),
        weight,
        out_weight[0],
        dec_embed,
        decoder_grad[0],
    )
    return result[None, None]


def solution(mesh):
    placed = (
        P("segment", "dp", "seq", None),
        P("segment", None),
        P("segment", None),
        P("segment", "dp", None),
        P("segment", "dp", None),
        P(),
        P("dp", "seq", None),
        P("segment", "dp", "seq", None),
        P("dp", None),
    )
    return jax.shard_map(
        on_device,
        mesh=mesh,
        in_specs=placed,
        out_specs=P("segment", "dp", "seq", None),
        check_vma=False,
    )
```

```python
import functools

import jax
import jax.numpy as jnp
from jax import lax
from jax.experimental import pallas as pl
from jax.experimental.pallas import tpu as pltpu
from jax.sharding import PartitionSpec as P

HEADS = 16
EPS = 1e-06
MESH = pl.DeviceIdType.MESH
F32 = jnp.float32
BF16 = jnp.bfloat16


def contract_last(left_side, right_side):
    return lax.dot_general(
        left_side, right_side, (((1,), (1,)), ((), ())), preferred_element_type=F32
    )


def contract_first(left_side, right_side):
    return lax.dot_general(
        left_side, right_side, (((0,), (0,)), ((), ())), preferred_element_type=F32
    )


def head_backward(query_rows, key_rows, value_rows, grad_out, scaling):
    rows = query_rows.shape[0]
    step = min(512, rows)
    query_grads = []
    key_grad = value_grad = None
    for at in range(0, rows, step):
        query = query_rows[at : at + step]
        grad = grad_out[at : at + step]
        scores = contract_last(query, key_rows) * scaling
        weights = jnp.exp(scores - jnp.max(scores, axis=1, keepdims=True))
        probs = weights * (1.0 / jnp.sum(weights, axis=1, keepdims=True))
        probs_low = probs.astype(BF16)
        output = jnp.dot(probs_low, value_rows, preferred_element_type=F32)
        row_delta = jnp.sum(grad.astype(F32) * output, axis=1, keepdims=True)
        grad_probs = contract_last(grad, value_rows)
        grad_scores = (probs * (grad_probs - row_delta)).astype(BF16)
        query_grads.append(
            (jnp.dot(grad_scores, key_rows, preferred_element_type=F32) * scaling).astype(BF16)
        )
        key_part = contract_first(grad_scores, query) * scaling
        value_part = contract_first(probs_low, grad)
        key_grad = key_part if key_grad is None else key_grad + key_part
        value_grad = value_part if value_grad is None else value_grad + value_part
    query_grad = query_grads[0] if len(query_grads) == 1 else jnp.concatenate(query_grads, axis=0)
    return query_grad, key_grad.astype(BF16), value_grad.astype(BF16)


def kernel(
    dims,
    x_ref, gain_ref, bias_ref, prev_ref, ids_ref, w_ref, ow_ref, de_ref, dg_ref,
    out_ref,
    wc, ow, de, dg, low, normed_ref, spread_ref, cot, go, ga, pk, pr, px,
    pa, pj, gp, ps, pn,
    lw_sem, lo_sem, prev_s, prev_r, w_s, w_r, pk_s, pk_r, px_s, px_r, l_s, l_r,
    g_s, g_r, b_s, b_r,
):
    dp, segs, groups, tok, width, chunks, pair, head_size, sliced = dims
    cw = pair * head_size
    hw = chunks * cw
    depth = width // dp
    per_dp = groups // dp
    d = lax.axis_index("dp")
    s = lax.axis_index("segment")
    z = lax.axis_index("seq")
    last = s == segs - 1
    owner = z // per_dp

    def z_at(o):
        return lax.rem(z + o, groups)

    def d_at(o):
        return lax.rem(d + o, dp)

    def remote(src, dst, send, recv, dd, ss, zz):
        return pltpu.make_async_remote_copy(
            src_ref=src, dst_ref=dst, send_sem=send, recv_sem=recv,
            device_id=(dd, ss, zz), device_id_type=MESH,
        )

    local_w = []
    if sliced:
        for ch in range(chunks):
            for part in range(3):
                at = pl.multiple_of(part * width + z * hw + ch * cw, 128)
                local_w.append(
                    pltpu.make_async_copy(
                        w_ref.at[:, pl.ds(at, cw)],
                        wc.at[d, ch, :, pl.ds(part * cw, cw)],
                        lw_sem.at[ch, part],
                    )
                )
    else:
        local_w.append(pltpu.make_async_copy(w_ref.at[z], wc.at[d], lw_sem.at[0, 0]))
    ow_copy = pltpu.make_async_copy(ow_ref, ow, lo_sem.at[0])
    de_copy = pltpu.make_async_copy(de_ref, de, lo_sem.at[1])
    dg_copy = pltpu.make_async_copy(dg_ref, dg, lo_sem.at[2])
    for copy in local_w:
        copy.start()

    @pl.when(last)
    def _():
        dg_copy.start()
        de_copy.start()

    ow_copy.start()

    barrier = pltpu.get_barrier_semaphore()
    for od in range(dp):
        for oz in range(groups):
            if od or oz:
                pl.semaphore_signal(
                    barrier, inc=1, device_id=(d_at(od), s, z_at(oz)), device_id_type=MESH
                )

    for od in range(dp):
        pl.semaphore_signal(
            barrier, inc=1, device_id=(d_at(od), lax.rem(s + 1, segs), z), device_id_type=MESH
        )
    pl.semaphore_wait(barrier, dp * groups - 1 + dp)

    down = jnp.maximum(s - 1, 0)

    def prev_copy(o):
        c = d_at(o)
        return remote(prev_ref, cot.at[d], prev_s.at[c], prev_r.at[d], c, down, z)

    @pl.when(s > 0)
    def _():
        for o in range(dp):
            prev_copy(o).start()

    def pick_copy(o):
        g = z_at(o)
        return remote(pk.at[g], pr.at[z], pk_s.at[g], pk_r.at[z], d, s, g)

    def arrive(dst, recv, dd, zz):
        remote(dst, dst, recv, recv, dd, s, zz).wait_recv()

    @pl.when(last)
    def _():
        dg_copy.wait()
        patches = dg.shape[0]
        patch_ids = lax.broadcasted_iota(jnp.int32, (patches, tok), 0) + z * patches
        for o in list(range(1, groups)) + [0]:
            g = z_at(o)
            hit = jnp.where(patch_ids == ids_ref[g], 1.0, 0.0).astype(BF16)
            rows = contract_first(hit, dg[...]).astype(BF16)
            if o:
                pk[g] = rows
                pick_copy(o).start()
            else:
                pr[z] = rows

    values = x_ref[...].astype(F32)
    center = values - jnp.mean(values, axis=1, keepdims=True)
    spread = jnp.sqrt(jnp.mean(center * center, axis=1, keepdims=True) + EPS)
    normed = center / spread
    normed_ref[...] = normed
    spread_ref[...] = jnp.broadcast_to(spread, spread_ref.shape)
    lowered = (normed * gain_ref[...] + bias_ref[...]).astype(BF16)
    for c in range(dp):
        low[z, c] = lowered[:, c * depth : (c + 1) * depth]

    def low_copy(o, p):
        c = d_at(p)
        return remote(
            low.at[z, c], low.at[z, c], l_s.at[z_at(o), c], l_r.at[z, c], d, s, z_at(o)
        )

    def low_arrive(p):
        c = d_at(p)
        for o in range(1, groups):
            arrive(low.at[z_at(o), c], l_r.at[z_at(o), c], d, z_at(o))

    for o in range(1, groups):
        low_copy(o, 0).start()

    def w_copy(o, ch):
        dd = d_at(o)
        return remote(wc.at[d, ch], wc.at[d, ch], w_s.at[dd, ch], w_r.at[d, ch], dd, s, z)

    for copy in local_w:
        copy.wait()

    @pl.when(s < segs - 1)
    def _():
        for o in range(1, dp):
            w_copy(o, 0).start()

    def px_copy(o):
        return remote(px.at[d], px.at[d], px_s.at[d_at(o)], px_r.at[d], d_at(o), s, z)

    @pl.when(last)
    def _():
        for o in range(1, groups):
            arrive(pr.at[z_at(o)], pk_r.at[z_at(o)], d, z_at(o))
        picked = pr[0].astype(F32)
        for g in range(1, groups):
            picked = picked + pr[g].astype(F32)
        px[d] = picked.astype(BF16)
        for o in range(1, dp):
            px_copy(o).start()
        for o in range(1, dp):
            w_copy(o, 0).start()
        de_copy.wait()

    def g_copy(c, j):
        g = d * per_dp + j
        return remote(go.at[c, j], ga.at[z], g_s.at[c, j], g_r.at[z], c, s, g)

    ow_copy.wait()
    for o in range(dp):
        c = d_at(o)

        @pl.when(s < segs - 1)
        def _():
            remote(
                prev_ref, cot.at[c], prev_s.at[c], prev_r.at[c], c, lax.rem(s + 1, segs), z
            ).wait_recv()

        @pl.when(last)
        def _():
            if o:
                arrive(px.at[c], px_r.at[c], c, z)
            cot[c] = contract_last(px[c], de[...]).astype(BF16)

        grads = contract_last(cot[c], ow[...]).astype(BF16)
        for j in range(per_dp):
            for ch in range(chunks):
                at = (j * chunks + ch) * cw
                go[c, j, ch] = grads[:, at : at + cw]
            if o:
                g_copy(c, j).start()
            else:
                mine = d * per_dp + j == z

                @pl.when(jnp.logical_not(mine))
                def _():
                    g_copy(c, j).start()

                @pl.when(mine)
                def _():
                    ga[z] = go[c, j]

    for p in range(1, dp):
        for o in range(1, groups):
            low_copy(o, p).start()
    for ch in range(1, chunks):
        for o in range(1, dp):
            w_copy(o, ch).start()
    low_arrive(0)
    for ch in range(chunks):
        pa[ch] = jnp.dot(
            low[:, d].reshape(groups * tok, depth), wc[d, ch], preferred_element_type=F32
        )

    def back_copy(o):
        g = z_at(o)
        return remote(ps.at[g], pn.at[z], b_s.at[g], b_r.at[z], d, s, g)

    scaling = head_size ** (-0.5)
    for ch in range(chunks):
        total = pa[ch]
        for o in range(1, dp):
            dd = d_at(o)
            if ch == 0:
                low_arrive(o)
            arrive(wc.at[dd, ch], w_r.at[dd, ch], dd, z)
            total = total + jnp.dot(
                low[:, dd].reshape(groups * tok, depth), wc[dd, ch], preferred_element_type=F32
            )
        pj[...] = total.astype(BF16)
        if ch == 0:
            for src in range(groups):
                @pl.when(jnp.logical_not(jnp.logical_and(owner == d, src == z)))
                def _():
                    arrive(ga.at[src], g_r.at[src], owner, src)
        grad_rows = ga[:, ch].reshape(groups * tok, cw)
        found = ([], [], [])
        for h in range(pair):
            parts = [
                pj[:, part * cw + h * head_size : part * cw + (h + 1) * head_size]
                for part in range(3)
            ]
            result = head_backward(
                *parts, grad_rows[:, h * head_size : (h + 1) * head_size], scaling
            )
            for part in range(3):
                found[part].append(result[part])
        for part in range(3):
            whole = found[part][0] if pair == 1 else jnp.concatenate(found[part], axis=1)
            gp[ch, :, :, part * cw : (part + 1) * cw] = whole.reshape(groups, tok, cw)

    def term(g, c):
        total = None
        for ch in range(chunks):
            part = contract_last(gp[ch, g], wc[c, ch])
            total = part if total is None else total + part
        return total

    for o in range(1, groups):
        g = z_at(o)
        for c in range(dp):
            ps[g, :, c * depth : (c + 1) * depth] = term(g, c).astype(BF16)
        back_copy(o).start()
    grad_norm = jnp.concatenate([term(z, c) for c in range(dp)], axis=1)
    for o in range(1, groups):
        g = z_at(o)
        arrive(pn.at[g], b_r.at[g], d, g)
        grad_norm = grad_norm + pn[g].astype(F32)
    scaled = grad_norm * gain_ref[...]
    normed = normed_ref[...]
    grad_in = (
        scaled
        - jnp.mean(scaled, axis=1, keepdims=True)
        - normed * jnp.mean(scaled * normed, axis=1, keepdims=True)
    ) / spread_ref[:, :1]
    out_ref[...] = (cot[d].astype(F32) + grad_in).astype(BF16)

    @pl.when(s > 0)
    def _():
        for o in range(dp):
            prev_copy(o).wait_send()

    @pl.when(last)
    def _():
        for o in range(1, groups):
            pick_copy(o).wait_send()
        for o in range(1, dp):
            px_copy(o).wait_send()

    for o in range(1, groups):
        for p in range(dp):
            low_copy(o, p).wait_send()
        back_copy(o).wait_send()
    for o in range(1, dp):
        for ch in range(chunks):
            w_copy(o, ch).wait_send()
    for o in range(dp):
        c = d_at(o)
        for j in range(per_dp):
            if o:
                g_copy(c, j).wait_send()
            else:
                @pl.when(d * per_dp + j != z)
                def _():
                    g_copy(c, j).wait_send()


def on_device(
    layer_inputs, ln_gain, ln_bias, qkv_weight, out_weight, dec_embed, decoder_grad, previous, visible
):
    dp = lax.axis_size("dp")
    segs = lax.axis_size("segment")
    groups = lax.axis_size("seq")
    tokens = layer_inputs[0, 0]
    tok, width = tokens.shape
    head_size = width // HEADS
    head_count = HEADS // groups
    pair = 2 if head_count % 2 == 0 else 1
    chunks = head_count // pair
    cw = pair * head_size
    depth = width // dp
    per_dp = groups // dp
    patches, dec = decoder_grad.shape[1:]
    sliced = cw % 128 == 0
    weight = qkv_weight[0]
    if not sliced:
        weight = weight.reshape(depth, 3, groups, chunks, cw).transpose(2, 3, 0, 1, 4)
        weight = weight.reshape(groups, chunks, depth, 3 * cw)
    dims = (dp, segs, groups, tok, width, chunks, pair, head_size, sliced)
    vmem = pl.BlockSpec(memory_space=pltpu.VMEM)
    anywhere = pl.BlockSpec(memory_space=pl.ANY)
    dma = pltpu.SemaphoreType.DMA
    result = pl.pallas_call(
        functools.partial(kernel, dims),
        out_shape=jax.ShapeDtypeStruct((tok, width), BF16),
        in_specs=[vmem] * 5 + [anywhere] * 4,
        out_specs=vmem,
        scratch_shapes=[
            pltpu.VMEM((dp, chunks, depth, 3 * cw), BF16),
            pltpu.VMEM((depth, width), BF16),
            pltpu.VMEM((width, dec), BF16),
            pltpu.VMEM((patches, dec), BF16),
            pltpu.VMEM((groups, dp, tok, depth), BF16),
            pltpu.VMEM((tok, width), F32),
            pltpu.VMEM((tok, 128), F32),
            pltpu.VMEM((dp, tok, width), BF16),
            pltpu.VMEM((dp, per_dp, chunks, tok, cw), BF16),
            pltpu.VMEM((groups, chunks, tok, cw), BF16),
            pltpu.VMEM((groups, tok, dec), BF16),
            pltpu.VMEM((groups, tok, dec), BF16),
            pltpu.VMEM((dp, tok, dec), BF16),
            pltpu.VMEM((chunks, groups * tok, 3 * cw), F32),
            pltpu.VMEM((groups * tok, 3 * cw), BF16),
            pltpu.VMEM((chunks, groups, tok, 3 * cw), BF16),
            pltpu.VMEM((groups, tok, width), BF16),
            pltpu.VMEM((groups, tok, width), BF16),
            dma((chunks, 3)),
            dma((3,)),
            dma((dp,)),
            dma((dp,)),
            dma((dp, chunks)),
            dma((dp, chunks)),
            dma((groups,)),
            dma((groups,)),
            dma((dp,)),
            dma((dp,)),
            dma((groups, dp)),
            dma((groups, dp)),
            dma((dp, per_dp)),
            dma((groups,)),
            dma((groups,)),
            dma((groups,)),
        ],
        compiler_params=pltpu.CompilerParams(
            collective_id=0, has_side_effects=True, vmem_limit_bytes=56 * 1024 * 1024
        ),
    )(
        tokens,
        ln_gain,
        ln_bias,
        previous[0, 0],
        visible[0].reshape(groups, 1, tok),
        weight,
        out_weight[0],
        dec_embed,
        decoder_grad[0],
    )
    return result[None, None]


def solution(mesh):
    placed = (
        P("segment", "dp", "seq", None),
        P("segment", None),
        P("segment", None),
        P("segment", "dp", None),
        P("segment", "dp", None),
        P(),
        P("dp", "seq", None),
        P("segment", "dp", "seq", None),
        P("dp", None),
    )
    return jax.shard_map(
        on_device,
        mesh=mesh,
        in_specs=placed,
        out_specs=P("segment", "dp", "seq", None),
        check_vma=False,
    )
```

```python
import functools

import jax
import jax.numpy as jnp
from jax import lax
from jax.experimental import pallas as pl
from jax.experimental.pallas import tpu as pltpu
from jax.sharding import PartitionSpec as P

HEADS = 16
EPS = 1e-06
MESH = pl.DeviceIdType.MESH
F32 = jnp.float32
BF16 = jnp.bfloat16


def contract_last(left_side, right_side):
    return lax.dot_general(
        left_side, right_side, (((1,), (1,)), ((), ())), preferred_element_type=F32
    )


def contract_first(left_side, right_side):
    return lax.dot_general(
        left_side, right_side, (((0,), (0,)), ((), ())), preferred_element_type=F32
    )


def head_backward(query_rows, key_rows, value_rows, grad_out, scaling):
    rows = query_rows.shape[0]
    step = min(512, rows)
    query_grads = []
    key_grad = value_grad = None
    for at in range(0, rows, step):
        query = query_rows[at : at + step]
        grad = grad_out[at : at + step]
        scores = contract_last(query, key_rows) * scaling
        weights = jnp.exp(scores - jnp.max(scores, axis=1, keepdims=True))
        probs = weights * (1.0 / jnp.sum(weights, axis=1, keepdims=True))
        probs_low = probs.astype(BF16)
        output = jnp.dot(probs_low, value_rows, preferred_element_type=F32)
        row_delta = jnp.sum(grad.astype(F32) * output, axis=1, keepdims=True)
        grad_probs = contract_last(grad, value_rows)
        grad_scores = (probs * (grad_probs - row_delta)).astype(BF16)
        query_grads.append(
            (jnp.dot(grad_scores, key_rows, preferred_element_type=F32) * scaling).astype(BF16)
        )
        key_part = contract_first(grad_scores, query) * scaling
        value_part = contract_first(probs_low, grad)
        key_grad = key_part if key_grad is None else key_grad + key_part
        value_grad = value_part if value_grad is None else value_grad + value_part
    query_grad = query_grads[0] if len(query_grads) == 1 else jnp.concatenate(query_grads, axis=0)
    return query_grad, key_grad.astype(BF16), value_grad.astype(BF16)


def kernel(
    dims,
    x_ref, gain_ref, bias_ref, prev_ref, ids_ref, w_ref, ow_ref, de_ref, dg_ref,
    out_ref,
    wc, ow, de, dg, low, normed_ref, spread_ref, cot, go, ga, pk, pr, px,
    pa, pj, gp, ps, pn,
    lw_sem, lo_sem, prev_s, prev_r, w_s, w_r, pk_s, pk_r, px_s, px_r, l_s, l_r,
    g_s, g_r, b_s, b_r,
):
    dp, segs, groups, tok, width, chunks, pair, head_size, sliced = dims
    cw = pair * head_size
    hw = chunks * cw
    depth = width // dp
    per_dp = groups // dp
    d = lax.axis_index("dp")
    s = lax.axis_index("segment")
    z = lax.axis_index("seq")
    last = s == segs - 1
    owner = z // per_dp

    def z_at(o):
        return lax.rem(z + o, groups)

    def d_at(o):
        return lax.rem(d + o, dp)

    def remote(src, dst, send, recv, dd, ss, zz):
        return pltpu.make_async_remote_copy(
            src_ref=src, dst_ref=dst, send_sem=send, recv_sem=recv,
            device_id=(dd, ss, zz), device_id_type=MESH,
        )

    local_w = []
    if sliced:
        for ch in range(chunks):
            for part in range(3):
                at = pl.multiple_of(part * width + z * hw + ch * cw, 128)
                local_w.append(
                    pltpu.make_async_copy(
                        w_ref.at[:, pl.ds(at, cw)],
                        wc.at[d, ch, :, pl.ds(part * cw, cw)],
                        lw_sem.at[ch, part],
                    )
                )
    else:
        local_w.append(pltpu.make_async_copy(w_ref.at[z], wc.at[d], lw_sem.at[0, 0]))
    ow_copy = pltpu.make_async_copy(ow_ref, ow, lo_sem.at[0])
    de_copy = pltpu.make_async_copy(de_ref, de, lo_sem.at[1])
    dg_copy = pltpu.make_async_copy(dg_ref, dg, lo_sem.at[2])
    for copy in local_w:
        copy.start()

    @pl.when(last)
    def _():
        dg_copy.start()
        de_copy.start()

    ow_copy.start()

    barrier = pltpu.get_barrier_semaphore()
    for od in range(dp):
        for oz in range(groups):
            if od or oz:
                pl.semaphore_signal(
                    barrier, inc=1, device_id=(d_at(od), s, z_at(oz)), device_id_type=MESH
                )

    for od in range(dp):
        pl.semaphore_signal(
            barrier, inc=1, device_id=(d_at(od), lax.rem(s + 1, segs), z), device_id_type=MESH
        )
    values = x_ref[...].astype(F32)
    center = values - jnp.mean(values, axis=1, keepdims=True)
    spread = jnp.sqrt(jnp.mean(center * center, axis=1, keepdims=True) + EPS)
    normed = center / spread
    normed_ref[...] = normed
    spread_ref[...] = jnp.broadcast_to(spread, spread_ref.shape)
    lowered = (normed * gain_ref[...] + bias_ref[...]).astype(BF16)
    for c in range(dp):
        low[z, c] = lowered[:, c * depth : (c + 1) * depth]

    pl.semaphore_wait(barrier, dp * groups - 1 + dp)

    down = jnp.maximum(s - 1, 0)

    def prev_copy(o):
        c = d_at(o)
        return remote(prev_ref, cot.at[d], prev_s.at[c], prev_r.at[d], c, down, z)

    @pl.when(s > 0)
    def _():
        for o in range(dp):
            prev_copy(o).start()

    def pick_copy(o):
        g = z_at(o)
        return remote(pk.at[g], pr.at[z], pk_s.at[g], pk_r.at[z], d, s, g)

    def arrive(dst, recv, dd, zz):
        remote(dst, dst, recv, recv, dd, s, zz).wait_recv()

    @pl.when(last)
    def _():
        dg_copy.wait()
        patches = dg.shape[0]
        patch_ids = lax.broadcasted_iota(jnp.int32, (patches, tok), 0) + z * patches
        for o in list(range(1, groups)) + [0]:
            g = z_at(o)
            hit = jnp.where(patch_ids == ids_ref[g], 1.0, 0.0).astype(BF16)
            rows = contract_first(hit, dg[...]).astype(BF16)
            if o:
                pk[g] = rows
                pick_copy(o).start()
            else:
                pr[z] = rows

    def low_copy(src, p, way):
        c = d_at(p)
        return remote(
            low.at[src, c], low.at[src, c], l_s.at[way, src, c], l_r.at[src, c],
            d, s, z + 1 - 2 * way,
        )

    def low_step(p, way, k, act):
        src = z - k if way == 0 else z + k
        here = src >= 0 if way == 0 else src < groups
        onward = z < groups - 1 if way == 0 else z > 0
        if k and act == "start":
            @pl.when(here)
            def _():
                arrive(low.at[src, d_at(p)], l_r.at[src, d_at(p)], d, src)

        @pl.when(jnp.logical_and(here, onward))
        def _():
            if act == "start":
                low_copy(src, p, way).start()
            else:
                low_copy(src, p, way).wait_send()

    def low_relay(k, act="start"):
        for p in range(dp):
            for way in range(2):
                low_step(p, way, k, act)

    low_relay(0)

    def w_copy(o, ch):
        dd = d_at(o)
        return remote(wc.at[d, ch], wc.at[d, ch], w_s.at[dd, ch], w_r.at[d, ch], dd, s, z)

    for copy in local_w:
        copy.wait()

    @pl.when(s < segs - 1)
    def _():
        for o in range(1, dp):
            w_copy(o, 0).start()

    def px_copy(o):
        return remote(px.at[d], px.at[d], px_s.at[d_at(o)], px_r.at[d], d_at(o), s, z)

    @pl.when(last)
    def _():
        for o in range(1, groups):
            arrive(pr.at[z_at(o)], pk_r.at[z_at(o)], d, z_at(o))
        picked = pr[0].astype(F32)
        for g in range(1, groups):
            picked = picked + pr[g].astype(F32)
        px[d] = picked.astype(BF16)
        for o in range(1, dp):
            px_copy(o).start()
        for o in range(1, dp):
            w_copy(o, 0).start()
        de_copy.wait()

    low_relay(1)

    def g_copy(c, j):
        g = d * per_dp + j
        return remote(go.at[c, j], ga.at[z], g_s.at[c, j], g_r.at[z], c, s, g)

    ow_copy.wait()
    for o in range(dp):
        c = d_at(o)

        @pl.when(s < segs - 1)
        def _():
            remote(
                prev_ref, cot.at[c], prev_s.at[c], prev_r.at[c], c, lax.rem(s + 1, segs), z
            ).wait_recv()

        @pl.when(last)
        def _():
            if o:
                arrive(px.at[c], px_r.at[c], c, z)
            cot[c] = contract_last(px[c], de[...]).astype(BF16)

        grads = contract_last(cot[c], ow[...]).astype(BF16)
        for j in range(per_dp):
            for ch in range(chunks):
                at = (j * chunks + ch) * cw
                go[c, j, ch] = grads[:, at : at + cw]
            if o:
                g_copy(c, j).start()
            else:
                mine = d * per_dp + j == z

                @pl.when(jnp.logical_not(mine))
                def _():
                    g_copy(c, j).start()

                @pl.when(mine)
                def _():
                    ga[z] = go[c, j]

    for ch in range(1, chunks):
        for o in range(1, dp):
            w_copy(o, ch).start()
    for k in range(2, groups):
        low_relay(k)
    for ch in range(chunks):
        pa[ch] = jnp.dot(
            low[:, d].reshape(groups * tok, depth), wc[d, ch], preferred_element_type=F32
        )

    def back_copy(o):
        g = z_at(o)
        return remote(ps.at[g], pn.at[z], b_s.at[g], b_r.at[z], d, s, g)

    scaling = head_size ** (-0.5)
    for ch in range(chunks):
        total = pa[ch]
        for o in range(1, dp):
            dd = d_at(o)
            arrive(wc.at[dd, ch], w_r.at[dd, ch], dd, z)
            total = total + jnp.dot(
                low[:, dd].reshape(groups * tok, depth), wc[dd, ch], preferred_element_type=F32
            )
        pj[...] = total.astype(BF16)
        if ch == 0:
            for src in range(groups):
                @pl.when(jnp.logical_not(jnp.logical_and(owner == d, src == z)))
                def _():
                    arrive(ga.at[src], g_r.at[src], owner, src)
        grad_rows = ga[:, ch].reshape(groups * tok, cw)
        found = ([], [], [])
        for h in range(pair):
            parts = [
                pj[:, part * cw + h * head_size : part * cw + (h + 1) * head_size]
                for part in range(3)
            ]
            result = head_backward(
                *parts, grad_rows[:, h * head_size : (h + 1) * head_size], scaling
            )
            for part in range(3):
                found[part].append(result[part])
        for part in range(3):
            whole = found[part][0] if pair == 1 else jnp.concatenate(found[part], axis=1)
            gp[ch, :, :, part * cw : (part + 1) * cw] = whole.reshape(groups, tok, cw)

    def term(g, c):
        total = None
        for ch in range(chunks):
            part = contract_last(gp[ch, g], wc[c, ch])
            total = part if total is None else total + part
        return total

    for o in range(1, groups):
        g = z_at(o)
        for c in range(dp):
            ps[g, :, c * depth : (c + 1) * depth] = term(g, c).astype(BF16)
        back_copy(o).start()
    grad_norm = jnp.concatenate([term(z, c) for c in range(dp)], axis=1)
    for o in range(1, groups):
        g = z_at(o)
        arrive(pn.at[g], b_r.at[g], d, g)
        grad_norm = grad_norm + pn[g].astype(F32)
    scaled = grad_norm * gain_ref[...]
    normed = normed_ref[...]
    grad_in = (
        scaled
        - jnp.mean(scaled, axis=1, keepdims=True)
        - normed * jnp.mean(scaled * normed, axis=1, keepdims=True)
    ) / spread_ref[:, :1]
    out_ref[...] = (cot[d].astype(F32) + grad_in).astype(BF16)

    @pl.when(s > 0)
    def _():
        for o in range(dp):
            prev_copy(o).wait_send()

    @pl.when(last)
    def _():
        for o in range(1, groups):
            pick_copy(o).wait_send()
        for o in range(1, dp):
            px_copy(o).wait_send()

    for o in range(1, groups):
        back_copy(o).wait_send()
    for k in range(groups - 1):
        low_relay(k, 'wait')
    for o in range(1, dp):
        for ch in range(chunks):
            w_copy(o, ch).wait_send()
    for o in range(dp):
        c = d_at(o)
        for j in range(per_dp):
            if o:
                g_copy(c, j).wait_send()
            else:
                @pl.when(d * per_dp + j != z)
                def _():
                    g_copy(c, j).wait_send()


def on_device(
    layer_inputs, ln_gain, ln_bias, qkv_weight, out_weight, dec_embed, decoder_grad, previous, visible
):
    dp = lax.axis_size("dp")
    segs = lax.axis_size("segment")
    groups = lax.axis_size("seq")
    tokens = layer_inputs[0, 0]
    tok, width = tokens.shape
    head_size = width // HEADS
    head_count = HEADS // groups
    pair = 2 if head_count % 2 == 0 else 1
    chunks = head_count // pair
    cw = pair * head_size
    depth = width // dp
    per_dp = groups // dp
    patches, dec = decoder_grad.shape[1:]
    sliced = cw % 128 == 0
    weight = qkv_weight[0]
    if not sliced:
        weight = weight.reshape(depth, 3, groups, chunks, cw).transpose(2, 3, 0, 1, 4)
        weight = weight.reshape(groups, chunks, depth, 3 * cw)
    dims = (dp, segs, groups, tok, width, chunks, pair, head_size, sliced)
    vmem = pl.BlockSpec(memory_space=pltpu.VMEM)
    anywhere = pl.BlockSpec(memory_space=pl.ANY)
    dma = pltpu.SemaphoreType.DMA
    result = pl.pallas_call(
        functools.partial(kernel, dims),
        out_shape=jax.ShapeDtypeStruct((tok, width), BF16),
        in_specs=[vmem] * 3 + [anywhere, vmem] + [anywhere] * 4,
        out_specs=vmem,
        scratch_shapes=[
            pltpu.VMEM((dp, chunks, depth, 3 * cw), BF16),
            pltpu.VMEM((depth, width), BF16),
            pltpu.VMEM((width, dec), BF16),
            pltpu.VMEM((patches, dec), BF16),
            pltpu.VMEM((groups, dp, tok, depth), BF16),
            pltpu.VMEM((tok, width), F32),
            pltpu.VMEM((tok, 128), F32),
            pltpu.VMEM((dp, tok, width), BF16),
            pltpu.VMEM((dp, per_dp, chunks, tok, cw), BF16),
            pltpu.VMEM((groups, chunks, tok, cw), BF16),
            pltpu.VMEM((groups, tok, dec), BF16),
            pltpu.VMEM((groups, tok, dec), BF16),
            pltpu.VMEM((dp, tok, dec), BF16),
            pltpu.VMEM((chunks, groups * tok, 3 * cw), F32),
            pltpu.VMEM((groups * tok, 3 * cw), BF16),
            pltpu.VMEM((chunks, groups, tok, 3 * cw), BF16),
            pltpu.VMEM((groups, tok, width), BF16),
            pltpu.VMEM((groups, tok, width), BF16),
            dma((chunks, 3)),
            dma((3,)),
            dma((dp,)),
            dma((dp,)),
            dma((dp, chunks)),
            dma((dp, chunks)),
            dma((groups,)),
            dma((groups,)),
            dma((dp,)),
            dma((dp,)),
            dma((2, groups, dp)),
            dma((groups, dp)),
            dma((dp, per_dp)),
            dma((groups,)),
            dma((groups,)),
            dma((groups,)),
        ],
        compiler_params=pltpu.CompilerParams(
            collective_id=0, has_side_effects=True, vmem_limit_bytes=56 * 1024 * 1024
        ),
    )(
        tokens,
        ln_gain,
        ln_bias,
        previous[0, 0],
        visible[0].reshape(groups, 1, tok),
        weight,
        out_weight[0],
        dec_embed,
        decoder_grad[0],
    )
    return result[None, None]


def solution(mesh):
    placed = (
        P("segment", "dp", "seq", None),
        P("segment", None),
        P("segment", None),
        P("segment", "dp", None),
        P("segment", "dp", None),
        P(),
        P("dp", "seq", None),
        P("segment", "dp", "seq", None),
        P("dp", None),
    )
    return jax.shard_map(
        on_device,
        mesh=mesh,
        in_specs=placed,
        out_specs=P("segment", "dp", "seq", None),
        check_vma=False,
    )
```

```python
import functools

import jax
import jax.numpy as jnp
from jax import lax
from jax.experimental import pallas as pl
from jax.experimental.pallas import tpu as pltpu
from jax.sharding import PartitionSpec as P

HEADS = 16
EPS = 1e-06
MESH = pl.DeviceIdType.MESH
F32 = jnp.float32
BF16 = jnp.bfloat16


def contract_last(left_side, right_side):
    return lax.dot_general(
        left_side, right_side, (((1,), (1,)), ((), ())), preferred_element_type=F32
    )


def contract_first(left_side, right_side):
    return lax.dot_general(
        left_side, right_side, (((0,), (0,)), ((), ())), preferred_element_type=F32
    )


def head_backward(query_rows, key_rows, value_rows, grad_out, scaling):
    rows = query_rows.shape[0]
    step = min(512, rows)
    query_grads = []
    key_grad = value_grad = None
    for at in range(0, rows, step):
        query = query_rows[at : at + step]
        grad = grad_out[at : at + step]
        scores = contract_last(query, key_rows) * scaling
        weights = jnp.exp(scores - jnp.max(scores, axis=1, keepdims=True))
        probs = weights * (1.0 / jnp.sum(weights, axis=1, keepdims=True))
        probs_low = probs.astype(BF16)
        output = jnp.dot(probs_low, value_rows, preferred_element_type=F32)
        row_delta = jnp.sum(grad.astype(F32) * output, axis=1, keepdims=True)
        grad_probs = contract_last(grad, value_rows)
        grad_scores = (probs * (grad_probs - row_delta)).astype(BF16)
        query_grads.append(
            (jnp.dot(grad_scores, key_rows, preferred_element_type=F32) * scaling).astype(BF16)
        )
        key_part = contract_first(grad_scores, query) * scaling
        value_part = contract_first(probs_low, grad)
        key_grad = key_part if key_grad is None else key_grad + key_part
        value_grad = value_part if value_grad is None else value_grad + value_part
    query_grad = query_grads[0] if len(query_grads) == 1 else jnp.concatenate(query_grads, axis=0)
    return query_grad, key_grad.astype(BF16), value_grad.astype(BF16)


def kernel(
    dims,
    x_ref, gain_ref, bias_ref, prev_ref, ids_ref, w_ref, ow_ref, de_ref, dg_ref,
    out_ref,
    wc, ow, de, dg, low, normed_ref, spread_ref, cot, go, ga, pk, pr, px,
    pa, pj, gp, ps, pn,
    lw_sem, lo_sem, prev_s, prev_r, w_s, w_r, pk_s, pk_r, px_s, px_r, l_s, l_r,
    g_s, g_r, b_s, b_r,
):
    dp, segs, groups, tok, width, chunks, pair, head_size, sliced = dims
    cw = pair * head_size
    hw = chunks * cw
    depth = width // dp
    per_dp = groups // dp
    d = lax.axis_index("dp")
    s = lax.axis_index("segment")
    z = lax.axis_index("seq")
    last = s == segs - 1
    owner = z // per_dp

    def z_at(o):
        return lax.rem(z + o, groups)

    def d_at(o):
        return lax.rem(d + o, dp)

    def remote(src, dst, send, recv, dd, ss, zz):
        return pltpu.make_async_remote_copy(
            src_ref=src, dst_ref=dst, send_sem=send, recv_sem=recv,
            device_id=(dd, ss, zz), device_id_type=MESH,
        )

    local_w = []
    if sliced:
        for ch in range(chunks):
            for part in range(3):
                at = pl.multiple_of(part * width + z * hw + ch * cw, 128)
                local_w.append(
                    pltpu.make_async_copy(
                        w_ref.at[:, pl.ds(at, cw)],
                        wc.at[d, ch, :, pl.ds(part * cw, cw)],
                        lw_sem.at[ch, part],
                    )
                )
    else:
        local_w.append(pltpu.make_async_copy(w_ref.at[z], wc.at[d], lw_sem.at[0, 0]))
    ow_copy = pltpu.make_async_copy(ow_ref, ow, lo_sem.at[0])
    de_copy = pltpu.make_async_copy(de_ref, de, lo_sem.at[1])
    dg_copy = pltpu.make_async_copy(dg_ref, dg, lo_sem.at[2])
    for copy in local_w:
        copy.start()

    @pl.when(last)
    def _():
        dg_copy.start()
        de_copy.start()

    ow_copy.start()

    barrier = pltpu.get_barrier_semaphore()
    for od in range(dp):
        for oz in range(groups):
            if od or oz:
                pl.semaphore_signal(
                    barrier, inc=1, device_id=(d_at(od), s, z_at(oz)), device_id_type=MESH
                )

    for od in range(dp):
        pl.semaphore_signal(
            barrier, inc=1, device_id=(d_at(od), lax.rem(s + 1, segs), z), device_id_type=MESH
        )
    def meets(block, g):
        few, most, rows = tok // 8, 15 * tok // 8, groups * tok
        first = jnp.maximum(block * few, rows - (groups - block) * most)
        end = jnp.minimum((block + 1) * most, rows - (groups - 1 - block) * few)
        return jnp.logical_and(first < (g + 1) * tok, end > g * tok)

    @pl.when(last)
    def _():
        dg_copy.wait()
        patches = dg.shape[0]
        patch_ids = lax.broadcasted_iota(jnp.int32, (patches, tok), 0) + z * patches
        for o in list(range(1, groups)) + [0]:
            g = z_at(o)

            @pl.when(meets(z, g))
            def _():
                hit = jnp.where(patch_ids == ids_ref[g], 1.0, 0.0).astype(BF16)
                rows = contract_first(hit, dg[...]).astype(BF16)
                if o:
                    pk[g] = rows
                else:
                    pr[z] = rows

    values = x_ref[...].astype(F32)
    center = values - jnp.mean(values, axis=1, keepdims=True)
    spread = jnp.sqrt(jnp.mean(center * center, axis=1, keepdims=True) + EPS)
    normed = center / spread
    normed_ref[...] = normed
    spread_ref[...] = jnp.broadcast_to(spread, spread_ref.shape)
    lowered = (normed * gain_ref[...] + bias_ref[...]).astype(BF16)
    for c in range(dp):
        low[z, c] = lowered[:, c * depth : (c + 1) * depth]

    pl.semaphore_wait(barrier, dp * groups - 1 + dp)

    down = jnp.maximum(s - 1, 0)

    def prev_copy(o):
        c = d_at(o)
        return remote(prev_ref, cot.at[d], prev_s.at[c], prev_r.at[d], c, down, z)

    @pl.when(s > 0)
    def _():
        for o in range(dp):
            prev_copy(o).start()

    def pick_copy(o):
        g = z_at(o)
        return remote(pk.at[g], pr.at[z], pk_s.at[g], pk_r.at[z], d, s, g)

    def arrive(dst, recv, dd, zz):
        remote(dst, dst, recv, recv, dd, s, zz).wait_recv()

    @pl.when(last)
    def _():
        for o in range(1, groups):
            @pl.when(meets(z, z_at(o)))
            def _():
                pick_copy(o).start()

    def low_copy(src, p, way):
        c = d_at(p)
        return remote(
            low.at[src, c], low.at[src, c], l_s.at[way, src, c], l_r.at[src, c],
            d, s, z + 1 - 2 * way,
        )

    def low_step(p, way, k, act):
        src = z - k if way == 0 else z + k
        here = src >= 0 if way == 0 else src < groups
        onward = z < groups - 1 if way == 0 else z > 0
        if k and act == "start":
            @pl.when(here)
            def _():
                arrive(low.at[src, d_at(p)], l_r.at[src, d_at(p)], d, src)

        @pl.when(jnp.logical_and(here, onward))
        def _():
            if act == "start":
                low_copy(src, p, way).start()
            else:
                low_copy(src, p, way).wait_send()

    def low_relay(k, act="start"):
        for p in range(dp):
            for way in range(2):
                low_step(p, way, k, act)

    low_relay(0)

    def w_copy(o, ch):
        dd = d_at(o)
        return remote(wc.at[d, ch], wc.at[d, ch], w_s.at[dd, ch], w_r.at[d, ch], dd, s, z)

    for copy in local_w:
        copy.wait()

    @pl.when(s < segs - 1)
    def _():
        for o in range(1, dp):
            w_copy(o, 0).start()

    def px_copy(o):
        return remote(px.at[d], px.at[d], px_s.at[d_at(o)], px_r.at[d], d_at(o), s, z)

    @pl.when(last)
    def _():
        for o in range(1, groups):
            g = z_at(o)

            @pl.when(meets(g, z))
            def _():
                arrive(pr.at[g], pk_r.at[g], d, g)

            @pl.when(jnp.logical_not(meets(g, z)))
            def _():
                pr[g] = jnp.zeros(pr.shape[1:], BF16)

        picked = pr[0].astype(F32)
        for g in range(1, groups):
            picked = picked + pr[g].astype(F32)
        px[d] = picked.astype(BF16)
        for o in range(1, dp):
            px_copy(o).start()
        for o in range(1, dp):
            w_copy(o, 0).start()
        de_copy.wait()

    low_relay(1)

    def g_copy(c, j):
        g = d * per_dp + j
        return remote(go.at[c, j], ga.at[z], g_s.at[c, j], g_r.at[z], c, s, g)

    ow_copy.wait()
    for o in range(dp):
        c = d_at(o)

        @pl.when(s < segs - 1)
        def _():
            remote(
                prev_ref, cot.at[c], prev_s.at[c], prev_r.at[c], c, lax.rem(s + 1, segs), z
            ).wait_recv()

        @pl.when(last)
        def _():
            if o:
                arrive(px.at[c], px_r.at[c], c, z)
            cot[c] = contract_last(px[c], de[...]).astype(BF16)

        grads = contract_last(cot[c], ow[...]).astype(BF16)
        for j in range(per_dp):
            for ch in range(chunks):
                at = (j * chunks + ch) * cw
                go[c, j, ch] = grads[:, at : at + cw]
            if o:
                g_copy(c, j).start()
            else:
                mine = d * per_dp + j == z

                @pl.when(jnp.logical_not(mine))
                def _():
                    g_copy(c, j).start()

                @pl.when(mine)
                def _():
                    ga[z] = go[c, j]

    for ch in range(1, chunks):
        for o in range(1, dp):
            w_copy(o, ch).start()
    for k in range(2, groups):
        low_relay(k)
    for ch in range(chunks):
        pa[ch] = jnp.dot(
            low[:, d].reshape(groups * tok, depth), wc[d, ch], preferred_element_type=F32
        )

    def back_copy(o):
        g = z_at(o)
        return remote(ps.at[g], pn.at[z], b_s.at[g], b_r.at[z], d, s, g)

    scaling = head_size ** (-0.5)
    for ch in range(chunks):
        total = pa[ch]
        for o in range(1, dp):
            dd = d_at(o)
            arrive(wc.at[dd, ch], w_r.at[dd, ch], dd, z)
            total = total + jnp.dot(
                low[:, dd].reshape(groups * tok, depth), wc[dd, ch], preferred_element_type=F32
            )
        pj[...] = total.astype(BF16)
        if ch == 0:
            for src in range(groups):
                @pl.when(jnp.logical_not(jnp.logical_and(owner == d, src == z)))
                def _():
                    arrive(ga.at[src], g_r.at[src], owner, src)
        grad_rows = ga[:, ch].reshape(groups * tok, cw)
        found = ([], [], [])
        for h in range(pair):
            parts = [
                pj[:, part * cw + h * head_size : part * cw + (h + 1) * head_size]
                for part in range(3)
            ]
            result = head_backward(
                *parts, grad_rows[:, h * head_size : (h + 1) * head_size], scaling
            )
            for part in range(3):
                found[part].append(result[part])
        for part in range(3):
            whole = found[part][0] if pair == 1 else jnp.concatenate(found[part], axis=1)
            gp[ch, :, :, part * cw : (part + 1) * cw] = whole.reshape(groups, tok, cw)

    def term(g, c):
        total = None
        for ch in range(chunks):
            part = contract_last(gp[ch, g], wc[c, ch])
            total = part if total is None else total + part
        return total

    for o in range(1, groups):
        g = z_at(o)
        for c in range(dp):
            ps[g, :, c * depth : (c + 1) * depth] = term(g, c).astype(BF16)
        back_copy(o).start()
    grad_norm = jnp.concatenate([term(z, c) for c in range(dp)], axis=1)
    for o in range(1, groups):
        g = z_at(o)
        arrive(pn.at[g], b_r.at[g], d, g)
        grad_norm = grad_norm + pn[g].astype(F32)
    scaled = grad_norm * gain_ref[...]
    normed = normed_ref[...]
    grad_in = (
        scaled
        - jnp.mean(scaled, axis=1, keepdims=True)
        - normed * jnp.mean(scaled * normed, axis=1, keepdims=True)
    ) / spread_ref[:, :1]
    out_ref[...] = (cot[d].astype(F32) + grad_in).astype(BF16)

    @pl.when(s > 0)
    def _():
        for o in range(dp):
            prev_copy(o).wait_send()

    @pl.when(last)
    def _():
        for o in range(1, groups):
            @pl.when(meets(z, z_at(o)))
            def _():
                pick_copy(o).wait_send()

        for o in range(1, dp):
            px_copy(o).wait_send()

    for o in range(1, groups):
        back_copy(o).wait_send()
    for k in range(groups - 1):
        low_relay(k, 'wait')
    for o in range(1, dp):
        for ch in range(chunks):
            w_copy(o, ch).wait_send()
    for o in range(dp):
        c = d_at(o)
        for j in range(per_dp):
            if o:
                g_copy(c, j).wait_send()
            else:
                @pl.when(d * per_dp + j != z)
                def _():
                    g_copy(c, j).wait_send()


def on_device(
    layer_inputs, ln_gain, ln_bias, qkv_weight, out_weight, dec_embed, decoder_grad, previous, visible
):
    dp = lax.axis_size("dp")
    segs = lax.axis_size("segment")
    groups = lax.axis_size("seq")
    tokens = layer_inputs[0, 0]
    tok, width = tokens.shape
    head_size = width // HEADS
    head_count = HEADS // groups
    pair = 2 if head_count % 2 == 0 else 1
    chunks = head_count // pair
    cw = pair * head_size
    depth = width // dp
    per_dp = groups // dp
    patches, dec = decoder_grad.shape[1:]
    sliced = cw % 128 == 0
    weight = qkv_weight[0]
    if not sliced:
        weight = weight.reshape(depth, 3, groups, chunks, cw).transpose(2, 3, 0, 1, 4)
        weight = weight.reshape(groups, chunks, depth, 3 * cw)
    dims = (dp, segs, groups, tok, width, chunks, pair, head_size, sliced)
    vmem = pl.BlockSpec(memory_space=pltpu.VMEM)
    anywhere = pl.BlockSpec(memory_space=pl.ANY)
    dma = pltpu.SemaphoreType.DMA
    result = pl.pallas_call(
        functools.partial(kernel, dims),
        out_shape=jax.ShapeDtypeStruct((tok, width), BF16),
        in_specs=[vmem] * 3 + [anywhere, vmem] + [anywhere] * 4,
        out_specs=vmem,
        scratch_shapes=[
            pltpu.VMEM((dp, chunks, depth, 3 * cw), BF16),
            pltpu.VMEM((depth, width), BF16),
            pltpu.VMEM((width, dec), BF16),
            pltpu.VMEM((patches, dec), BF16),
            pltpu.VMEM((groups, dp, tok, depth), BF16),
            pltpu.VMEM((tok, width), F32),
            pltpu.VMEM((tok, 128), F32),
            pltpu.VMEM((dp, tok, width), BF16),
            pltpu.VMEM((dp, per_dp, chunks, tok, cw), BF16),
            pltpu.VMEM((groups, chunks, tok, cw), BF16),
            pltpu.VMEM((groups, tok, dec), BF16),
            pltpu.VMEM((groups, tok, dec), BF16),
            pltpu.VMEM((dp, tok, dec), BF16),
            pltpu.VMEM((chunks, groups * tok, 3 * cw), F32),
            pltpu.VMEM((groups * tok, 3 * cw), BF16),
            pltpu.VMEM((chunks, groups, tok, 3 * cw), BF16),
            pltpu.VMEM((groups, tok, width), BF16),
            pltpu.VMEM((groups, tok, width), BF16),
            dma((chunks, 3)),
            dma((3,)),
            dma((dp,)),
            dma((dp,)),
            dma((dp, chunks)),
            dma((dp, chunks)),
            dma((groups,)),
            dma((groups,)),
            dma((dp,)),
            dma((dp,)),
            dma((2, groups, dp)),
            dma((groups, dp)),
            dma((dp, per_dp)),
            dma((groups,)),
            dma((groups,)),
            dma((groups,)),
        ],
        compiler_params=pltpu.CompilerParams(
            collective_id=0, has_side_effects=True, vmem_limit_bytes=56 * 1024 * 1024
        ),
    )(
        tokens,
        ln_gain,
        ln_bias,
        previous[0, 0],
        visible[0].reshape(groups, 1, tok),
        weight,
        out_weight[0],
        dec_embed,
        decoder_grad[0],
    )
    return result[None, None]


def solution(mesh):
    placed = (
        P("segment", "dp", "seq", None),
        P("segment", None),
        P("segment", None),
        P("segment", "dp", None),
        P("segment", "dp", None),
        P(),
        P("dp", "seq", None),
        P("segment", "dp", "seq", None),
        P("dp", None),
    )
    return jax.shard_map(
        on_device,
        mesh=mesh,
        in_specs=placed,
        out_specs=P("segment", "dp", "seq", None),
        check_vma=False,
    )
```
